256 devices in a mesh: dp: 8 (over z), own: 32 (over y, x, core).
Axes of the slice: x: 4, y: 4, z: 8, core: 2. Of those that a mesh axis runs over, the one named last changes fastest.
Arguments:
- partials: bfloat16 [8, 96, 1024, 1024], P('dp', 'own'), may hold values from -0.125 to 0.125
- active_mask: int32 [96], replicated, may hold values from 0 to 1, as said below
- block_owner: int32 [96], replicated, may hold values from 0 to 31, as said below
- left_stats: float32 [64, 1024, 1024], P('own', 'dp'), may hold values from -6 to 6
- right_stats: float32 [64, 1024, 1024], P('own', 'dp'), may hold values from -6 to 6
- left_root: bfloat16 [64, 1024, 1024], P('own', 'dp'), may hold values from -0.4375 to 0.4375
- right_root: bfloat16 [64, 1024, 1024], P('own', 'dp'), may hold values from -0.4375 to 0.4375
Outputs:
- preconditioned: bfloat16 [96, 1024, 1024], P('own', 'dp')
- left_new: float32 [64, 1024, 1024], P('own', 'dp')
- right_new: float32 [64, 1024, 1024], P('own', 'dp')
The draws below stay inside these ranges and needn't reach their ends.
Inputs may be any that keep to these rules, and one draw needn't show every extreme that they name: `active_mask`: exactly 64 blocks are active. `block_owner`: every owner index owns exactly 3 blocks, and exactly 2 of them are active.
All inputs are finite; a program needn't handle non-finite values.
Results may differ from the reference program's by a relative error of at most 0.022.
Values may be sent and summed in bfloat16 or wider, within the bound.
No kernel may reach another device: no remote copies, remote signals or barrier semaphores. Data moves between devices by JAX's collectives and lax.ppermute only.
A program may use at most 128 MiB of HBM per device.

```python
import jax
import jax.numpy as jnp
from jax import lax

B = 1024
ACT = 2
BPD = 3
NB = 96
NACT = 64
N_DP = 8
N_OWN = 32


def block_order(key):
    return jax.random.permutation(key, NB).astype(jnp.int32)


def draw_active_mask(key, part):
    order = block_order(key)
    position = jnp.arange(NB, dtype=jnp.int32)
    values = (position % BPD < ACT).astype(jnp.int32)
    return jnp.zeros((NB,), jnp.int32).at[order].set(values)


def draw_block_owner(key, part):
    order = block_order(key)
    position = jnp.arange(NB, dtype=jnp.int32)
    values = (position // BPD).astype(jnp.int32)
    return jnp.zeros((NB,), jnp.int32).at[order].set(values)


def levels(stream_key, shape, split, low, high):
    factor_of = 1.0
    for dim, parts in split:
        steps = jax.random.uniform(jax.random.fold_in(jax.random.fold_in(stream_key, 6), dim), (parts,), jnp.float32, low / len(split), high / len(split))
        factor_of = factor_of * jnp.repeat(jnp.exp(steps), shape[dim] // parts).reshape((-1,) + (1,) * (len(shape) - 1 - dim))
    return factor_of


def centred(rng, dims, width, limit, split=(), kind=jnp.bfloat16):
    gain = levels(rng, dims, split, -0.22, 0.18) if split else 1.0
    drawn = jax.random.normal(rng, dims, jnp.float32) * width * gain
    return jnp.minimum(jnp.maximum(drawn, -limit), limit).astype(kind)


def setup_inputs(seed: int = 0) -> dict:
    streams_of = jax.random.split(jax.random.key(seed), 8)
    partials = centred(streams_of[0], (N_DP, NB, B, B), 0.02, 0.125, ((0, 8), (1, 32)))
    active_mask = draw_active_mask(jax.random.fold_in(streams_of[7], 71), 0)
    block_owner = draw_block_owner(jax.random.fold_in(streams_of[7], 71), 0)
    left_stats = centred(streams_of[3], (NACT, B, B), 1.0, 6.0, ((0, 32), (1, 8)), jnp.float32)
    right_stats = centred(streams_of[4], (NACT, B, B), 1.0, 6.0, ((0, 32), (1, 8)), jnp.float32)
    left_root = centred(streams_of[5], (NACT, B, B), (B // 6) ** -0.5, 0.4375, ((0, 32), (1, 8)))
    right_root = centred(streams_of[6], (NACT, B, B), (B // 6) ** -0.5, 0.4375, ((0, 32), (1, 8)))
    return {"partials": partials, "active_mask": active_mask, "block_owner": block_owner, "left_stats": left_stats, "right_stats": right_stats, "left_root": left_root, "right_root": right_root}


def slot_table(active_mask, block_owner, active_count, owners):
    block_total = active_mask.shape[0]
    index = jnp.arange(block_total, dtype=jnp.int32)
    live = active_mask == 1
    earlier = (block_owner[:, None] == block_owner[None, :]) & live[None, :] & (index[None, :] < index[:, None])
    slots = jnp.sum(earlier.astype(jnp.int32), axis=1)
    keyed = jnp.where(live, block_owner * active_count + slots, 0).astype(jnp.int32)
    targets = jnp.arange(owners * active_count, dtype=jnp.int32)
    hit = live[None, :] & (keyed[None, :] == targets[:, None])
    chosen = jnp.sum(jnp.where(hit, index[None, :], 0), axis=1).astype(jnp.int32)
    return keyed, live, chosen


def reference(partials, active_mask, block_owner, left_stats, right_stats, left_root, right_root):
    keyed, live, chosen = slot_table(active_mask, block_owner, ACT, N_OWN)

    def per_slot(target):
        block = lax.dynamic_index_in_dim(partials, chosen[target], 1, keepdims=False)
        gradient = jnp.sum(block.astype(jnp.float32), axis=0)
        left_one = left_stats[target] + jnp.dot(gradient, gradient.T, precision=lax.Precision.HIGHEST)
        right_one = right_stats[target] + jnp.dot(gradient.T, gradient, precision=lax.Precision.HIGHEST)
        mixed = jnp.dot(left_root[target], gradient.astype(jnp.bfloat16), preferred_element_type=jnp.float32).astype(jnp.bfloat16)
        result = jnp.dot(mixed, right_root[target], preferred_element_type=jnp.float32).astype(jnp.bfloat16)
        return left_one, right_one, result

    left_new, right_new, results = lax.map(per_slot, jnp.arange(NACT, dtype=jnp.int32))
    placed = jnp.take(results, keyed, axis=0)
    preconditioned = jnp.where(live[:, None, None], placed, jnp.zeros_like(placed))
    return preconditioned, left_new, right_new
```

```python
import jax
import jax.numpy as jnp
from jax import lax
from jax.experimental import pallas as pl
from jax.experimental.pallas import tpu as pltpu
from jax.sharding import PartitionSpec as P

TILE_ROWS = 16


def slot_table(active_mask, block_owner, active_count, owners):
    block_total = active_mask.shape[0]
    index = jnp.arange(block_total, dtype=jnp.int32)
    live = active_mask == 1
    earlier = (
        (block_owner[:, None] == block_owner[None, :])
        & live[None, :]
        & (index[None, :] < index[:, None])
    )
    slots = jnp.sum(earlier.astype(jnp.int32), axis=1)
    keyed = jnp.where(live, block_owner * active_count + slots, 0)
    targets = jnp.arange(owners * active_count, dtype=jnp.int32)
    hit = live[None, :] & (keyed[None, :] == targets[:, None])
    chosen = jnp.sum(jnp.where(hit, index[None, :], 0), axis=1)
    return (keyed, live, chosen)


def pick_kernel(table_ref, source_ref, out_ref):
    def step(t, carry):
        wanted = table_ref[t]
        block = source_ref[jnp.maximum(wanted, 0)]
        out_ref[t] = jnp.where(wanted >= 0, block, jnp.zeros_like(block))
        return carry

    lax.fori_loop(0, out_ref.shape[0], step, 0, unroll=4)


def pick(source, table):
    count = table.shape[0]
    shape = (count,) + source.shape[1:]
    return pl.pallas_call(
        pick_kernel,
        out_shape=jax.ShapeDtypeStruct(shape, source.dtype),
        in_specs=[
            pl.BlockSpec(memory_space=pltpu.SMEM),
            pl.BlockSpec(memory_space=pltpu.VMEM),
        ],
        out_specs=pl.BlockSpec(memory_space=pltpu.VMEM),
        compiler_params=pltpu.CompilerParams(vmem_limit_bytes=8 * 1024 * 1024),
        cost_estimate=pl.CostEstimate(
            flops=0, bytes_accessed=2 * (source.size + count * source[0].size), transcendentals=0
        ),
    )(table, source)


def to_pieces(slabs, owners):
    count, rows, cols = slabs.shape
    down = rows // TILE_ROWS
    across = owners // down
    split = slabs.reshape(count, down, TILE_ROWS, across, cols // across)
    return split.transpose(1, 3, 0, 2, 4).reshape(owners, count, TILE_ROWS, cols // across)


def from_pieces(pieces, rows, cols):
    owners, count = pieces.shape[:2]
    down = rows // TILE_ROWS
    across = owners // down
    split = pieces.reshape(down, across, count, TILE_ROWS, cols // across)
    return split.transpose(2, 0, 3, 1, 4).reshape(count, rows, cols)


def swap(pieces):
    return lax.all_to_all(pieces, "own", split_axis=0, concat_axis=0, tiled=True)


def local(partials, active_mask, block_owner, left_stats, right_stats, left_root, right_root):
    width = partials.shape[3]
    active_count, rows = left_stats.shape[:2]
    owners = lax.axis_size("own")
    keyed, live, chosen = slot_table(active_mask, block_owner, active_count, owners)
    wanted = jnp.where(live, keyed, -1)
    my_start = lax.axis_index("dp") * rows

    summed = lax.psum_scatter(partials[0], "dp", scatter_dimension=1, tiled=True)
    summed, right_root = lax.optimization_barrier((summed, right_root))
    right_full = lax.all_gather(right_root, "dp", axis=1, tiled=True)

    spread = swap(to_pieces(summed, owners))
    piece = spread.shape[2:]
    picked = pick(spread.reshape((-1,) + piece), chosen)
    arrived = swap(picked.reshape((owners, active_count) + piece))
    gradient = from_pieces(arrived, rows, width)
    full = lax.all_gather(gradient, "dp", axis=1, tiled=True)

    mixed = jnp.einsum(
        "arn,anw->arw", left_root, full, preferred_element_type=jnp.float32
    ).astype(jnp.bfloat16)
    result = jnp.einsum(
        "arn,anw->arw", mixed, right_full, preferred_element_type=jnp.float32
    ).astype(jnp.bfloat16)

    back = swap(to_pieces(result, owners))
    placed = pick(back.reshape((-1,) + piece), wanted)
    returned = swap(placed.reshape((owners, -1) + piece))
    preconditioned = from_pieces(returned, rows, width)

    left_new = left_stats + jnp.einsum(
        "arw,anw->arn", gradient, full, preferred_element_type=jnp.float32
    )
    mine = lax.dynamic_slice_in_dim(full, my_start, rows, 2)
    right_new = right_stats + jnp.einsum(
        "anr,anw->arw", mine, full, preferred_element_type=jnp.float32
    )
    return (preconditioned, left_new, right_new)


def solution(mesh):
    placed = (
        P("dp", "own", None, None),
        P(),
        P(),
        P("own", "dp", None),
        P("own", "dp", None),
        P("own", "dp", None),
        P("own", "dp", None),
    )
    return jax.shard_map(
        local,
        mesh=mesh,
        in_specs=placed,
        out_specs=(P("own", "dp", None), P("own", "dp", None), P("own", "dp", None)),
        check_vma=False,
    )
```

```python
import functools

import jax
import jax.numpy as jnp
from jax import lax
from jax.experimental import pallas as pl
from jax.experimental.pallas import tpu as pltpu
from jax.sharding import PartitionSpec as P

TILE_ROWS = 16
STREAMS = 2
F32 = jnp.float32
BF16 = jnp.bfloat16
MIB = 1024 * 1024
VMEM = pl.BlockSpec(memory_space=pltpu.VMEM)
SMEM = pl.BlockSpec(memory_space=pltpu.SMEM)
HBM = pl.BlockSpec(memory_space=pltpu.HBM)


def slot_table(active_mask, block_owner, active_count, owners):
    block_total = active_mask.shape[0]
    index = jnp.arange(block_total, dtype=jnp.int32)
    live = active_mask == 1
    earlier = (
        (block_owner[:, None] == block_owner[None, :])
        & live[None, :]
        & (index[None, :] < index[:, None])
    )
    slots = jnp.sum(earlier.astype(jnp.int32), axis=1)
    keyed = jnp.where(live, block_owner * active_count + slots, 0)
    targets = jnp.arange(owners * active_count, dtype=jnp.int32)
    hit = live[None, :] & (keyed[None, :] == targets[:, None])
    chosen = jnp.sum(jnp.where(hit, index[None, :], 0), axis=1)
    return (keyed, live, chosen)


def call(kernel, out_shape, in_specs, args, flops=0, scratch=(), limit=16, out_specs=None):
    outs = jax.tree.leaves(out_shape)
    whole = [x for x, spec in zip(args, in_specs) if spec is not HBM]
    moved = sum(x.size * x.dtype.itemsize for x in whole + outs)
    return pl.pallas_call(
        kernel,
        out_shape=out_shape,
        in_specs=in_specs,
        out_specs=out_specs or jax.tree.map(lambda _: VMEM, out_shape),
        scratch_shapes=list(scratch),
        compiler_params=pltpu.CompilerParams(vmem_limit_bytes=limit * MIB),
        cost_estimate=pl.CostEstimate(flops=flops, bytes_accessed=moved, transcendentals=0),
    )(*args)


def pick_kernel(table_ref, source_ref, out_ref):
    def step(t, carry):
        wanted = table_ref[t]
        block = source_ref[jnp.maximum(wanted, 0)]
        out_ref[t] = jnp.where(wanted >= 0, block, jnp.zeros_like(block))
        return carry

    lax.fori_loop(0, out_ref.shape[0], step, 0, unroll=8)


def pick(source, table):
    shape = jax.ShapeDtypeStruct(table.shape + source.shape[1:], source.dtype)
    return call(pick_kernel, shape, [SMEM, VMEM], (table, source))


def put_pieces(out_ref, item, value, first=0):
    rows, cols = value.shape
    narrow = out_ref.shape[3]
    across = cols // narrow
    for i in range(rows // TILE_ROWS):
        for j in range(across):
            out_ref[(first + i) * across + j, item] = value[
                i * TILE_ROWS : (i + 1) * TILE_ROWS, j * narrow : (j + 1) * narrow
            ]


def unpack_kernel(pieces_ref, *out_refs):
    owners, count, tall, narrow = pieces_ref.shape
    for item in range(count):
        if len(out_refs) == 1:
            out_ref = out_refs[0].at[item]
        else:
            out_ref = out_refs[item]
        across = out_ref.shape[1] // narrow
        for i in range(owners // across):
            for j in range(across):
                out_ref[i * tall : (i + 1) * tall, j * narrow : (j + 1) * narrow] = pieces_ref[
                    i * across + j, item
                ]


def add_kernel(got_ref, piece_ref, out_ref):
    out_ref[...] = (got_ref[...].astype(F32) + piece_ref[...].astype(F32)).astype(BF16)


def pack_kernel(own_ref, *rest):
    got, out_ref = rest[:-1], rest[-1]
    count, rows = own_ref.shape[:2]
    part = got[0].shape[1]
    for item in range(count):
        for stream in range(rows // part):
            total = own_ref[item, stream * part : (stream + 1) * part].astype(F32)
            for ref in got[2 * stream : 2 * stream + 2]:
                total = total + ref[item].astype(F32)
            put_pieces(out_ref, item, total.astype(BF16), stream * part // TILE_ROWS)


def hop(value, step, ring):
    return lax.ppermute(value, "dp", [(i, (i + step) % ring) for i in range(ring)])


def chains(count, ring):
    far, near = ring // 2, ring - 1 - ring // 2
    for step in range(far):
        for block in range(count):
            long_way = 1 if block % 2 == 0 else -1
            for way, length in ((long_way, far), (-long_way, near)):
                place = step - (far - length)
                if place >= 0:
                    yield block, way, place, length


def sum_over_ring(blocks, rows, owners):
    count, _, cols = blocks.shape
    ring = lax.axis_size("dp")
    me = lax.axis_index("dp").astype(jnp.int32)
    part = rows // STREAMS
    shape = (count, part, cols)
    order = list(chains(STREAMS, ring))

    def piece(me, stream, way, place, length):
        target = lax.rem(me + way * (length - place) + ring, ring)
        return lax.dynamic_slice(blocks, (0, target * rows + stream * part, 0), shape)

    first = {step[:2]: piece(me, *step) for step in order if step[2] == 0}
    later, first = lax.optimization_barrier((me, first))
    pieces = {step[:3]: piece(later, *step) for step in order if step[2] > 0}
    own = lax.dynamic_slice(blocks, (0, later * rows, 0), (count, rows, cols))
    held = {}
    for stream, way, place, length in order:
        if place == 0:
            value = first[stream, way]
        else:
            value = call(
                add_kernel,
                jax.ShapeDtypeStruct(shape, BF16),
                [VMEM, VMEM],
                (held[stream, way], pieces[stream, way, place]),
            )
        held[stream, way] = hop(value, way, ring)
    got = [held[stream, way] for stream in range(STREAMS) for way in (1, -1)]
    narrow = cols * (rows // TILE_ROWS) // owners
    return call(
        pack_kernel,
        jax.ShapeDtypeStruct((owners, count, TILE_ROWS, narrow), BF16),
        [VMEM] * (1 + len(got)),
        (own, *got),
    )


def columns(me, k, ring, width):
    return pl.ds(pl.multiple_of(lax.rem(me + k, ring) * width, width), width)


def mix_kernel(ring, places, me_ref, root_ref, *rest):
    shards, (old_ref, new_ref) = rest[: len(places)], rest[len(places) :]
    me = me_ref[0]
    rows = root_ref.shape[1]
    for a in range(root_ref.shape[0]):
        total = old_ref[a]
        for (block, k), shard in zip(places, shards):
            if block == a:
                total = total + jnp.dot(
                    root_ref[a, :, columns(me, k, ring, rows)],
                    shard[...],
                    preferred_element_type=F32,
                )
        new_ref[a] = total


def gram_kernel(ring, places, me_ref, *rest):
    shards, rest = rest[: len(places)], rest[len(places) :]
    owned, (left_in, right_in, left_ref, right_ref) = rest[:-4], rest[-4:]
    me = me_ref[0]
    rows = left_ref.shape[1]
    mine = columns(me, 0, ring, rows)
    left_ref[...] = left_in[...]
    for a in range(left_ref.shape[0]):
        total = right_in[a]
        for (block, k), shard in zip(places, shards):
            if block == a:
                cols = columns(me, k, ring, rows)
                left_ref[a, :, cols] = left_ref[a, :, cols] + lax.dot_general(
                    owned[a][...],
                    shard[...],
                    (((1,), (1,)), ((), ())),
                    preferred_element_type=F32,
                )
                total = total + lax.dot_general(
                    shard[:, mine],
                    shard[...],
                    (((0,), (0,)), ((), ())),
                    preferred_element_type=F32,
                )
        right_ref[a] = total


def result_kernel(ring, places, me_ref, root_ref, right_ref, *rest):
    count = len(places)
    shards, (old_ref, out_ref), rest = rest[:count], rest[count : count + 2], rest[count + 2 :]
    kept, sems = rest[:count], rest[count]
    copies = []
    for i in range(count):
        copies.append(pltpu.make_async_copy(shards[i], kept[i], sems.at[i]))
        copies[i].start()
    me = me_ref[0]
    rows = root_ref.shape[1]
    for a in range(root_ref.shape[0]):
        total = old_ref[a]
        for (block, k), shard in zip(places, shards):
            if block == a:
                total = total + jnp.dot(
                    root_ref[a, :, columns(me, k, ring, rows)],
                    shard[...],
                    preferred_element_type=F32,
                )
        result = jnp.dot(total.astype(BF16), right_ref[a], preferred_element_type=F32)
        put_pieces(out_ref, a, result.astype(BF16))
    for copy in copies:
        copy.wait()


def swap(pieces):
    return lax.all_to_all(pieces, "own", split_axis=0, concat_axis=0, tiled=True)


def local(partials, active_mask, block_owner, left_stats, right_stats, left_root, right_root):
    blocks, width = partials.shape[1], partials.shape[3]
    active_count, rows = left_stats.shape[:2]
    owners = lax.axis_size("own")
    ring = lax.axis_size("dp")
    me = lax.axis_index("dp").astype(jnp.int32)[None]
    keyed, live, chosen = slot_table(active_mask, block_owner, active_count, owners)
    wanted = jnp.where(live, keyed, -1)

    summed = sum_over_ring(partials[0], rows, owners)
    summed, right_root = lax.optimization_barrier((summed, right_root))
    right_full = lax.all_gather(right_root, "dp", axis=1, tiled=True)

    spread = swap(summed)
    piece = spread.shape[2:]
    picked = pick(spread.reshape((-1,) + piece), chosen)
    arrived = swap(picked.reshape((owners, active_count) + piece))
    slab = jax.ShapeDtypeStruct((rows, width), BF16)
    gradient = call(unpack_kernel, [slab] * active_count, [VMEM], (arrived,))
    gradient = list(gradient)

    flops = 2 * rows * rows * width
    slabs = jax.ShapeDtypeStruct((active_count, rows, width), F32)
    mixed = jnp.zeros(slabs.shape, F32)
    left_new, right_new = left_stats, right_stats

    def gram(places, shards, left, right):
        return call(
            functools.partial(gram_kernel, ring, places),
            [slabs, slabs],
            [SMEM] + [VMEM] * (len(shards) + active_count + 2),
            (me, *shards, *gradient, left, right),
            flops=2 * flops * len(shards),
        )

    held = {}
    places, shards = [(block, 0) for block in range(active_count)], list(gradient)
    for step in range(ring // 2):
        mixed = call(
            functools.partial(mix_kernel, ring, places),
            slabs,
            [SMEM, VMEM] + [VMEM] * (len(shards) + 1),
            (me, left_root, *shards, mixed),
            flops=flops * len(shards),
        )
        left_new, right_new = gram(places, shards, left_new, right_new)
        places, shards = [], []
        for block, way, place, length in chains(active_count, ring):
            if place == step:
                value = held.get((block, way), gradient[block])
                if step == ring // 2 - 1:
                    value, right_full = lax.optimization_barrier((value, right_full))
                held[block, way] = hop(value, way, ring)
                places.append((block, (-way * (place + 1)) % ring))
                shards.append(held[block, way])
    slab = jax.ShapeDtypeStruct((rows, width), BF16)
    result, *shards = call(
        functools.partial(result_kernel, ring, places),
        [jax.ShapeDtypeStruct((owners, active_count) + piece, BF16)] + [slab] * len(shards),
        [SMEM, VMEM, VMEM] + [VMEM] * (len(shards) + 1),
        (me, left_root, right_full, *shards, mixed),
        flops=flops * (len(shards) + ring * active_count),
        scratch=[pltpu.SemaphoreType.DMA((len(shards),))],
        limit=24,
        out_specs=[VMEM] + [HBM] * len(shards),
    )

    back = swap(result)
    placed = pick(back.reshape((-1,) + piece), wanted)
    returned = swap(placed.reshape((owners, blocks) + piece))
    preconditioned = call(
        unpack_kernel,
        jax.ShapeDtypeStruct((blocks, rows, width), BF16),
        [VMEM],
        (returned,),
    )

    left_new, right_new = gram(places, shards, left_new, right_new)
    return (preconditioned, left_new, right_new)


def solution(mesh):
    placed = (
        P("dp", "own", None, None),
        P(),
        P(),
        P("own", "dp", None),
        P("own", "dp", None),
        P("own", "dp", None),
        P("own", "dp", None),
    )
    return jax.shard_map(
        local,
        mesh=mesh,
        in_specs=placed,
        out_specs=(P("own", "dp", None), P("own", "dp", None), P("own", "dp", None)),
        check_vma=False,
    )
```

```python
import functools

import jax
import jax.numpy as jnp
from jax import lax
from jax.experimental import pallas as pl
from jax.experimental.pallas import tpu as pltpu
from jax.sharding import PartitionSpec as P

TILE_ROWS = 16
STREAMS = 2
F32 = jnp.float32
BF16 = jnp.bfloat16
MIB = 1024 * 1024
VMEM = pl.BlockSpec(memory_space=pltpu.VMEM)
SMEM = pl.BlockSpec(memory_space=pltpu.SMEM)
HBM = pl.BlockSpec(memory_space=pltpu.HBM)


def slot_table(active_mask, block_owner, active_count, owners):
    block_total = active_mask.shape[0]
    index = jnp.arange(block_total, dtype=jnp.int32)
    live = active_mask == 1
    earlier = (
        (block_owner[:, None] == block_owner[None, :])
        & live[None, :]
        & (index[None, :] < index[:, None])
    )
    slots = jnp.sum(earlier.astype(jnp.int32), axis=1)
    keyed = jnp.where(live, block_owner * active_count + slots, 0)
    targets = jnp.arange(owners * active_count, dtype=jnp.int32)
    hit = live[None, :] & (keyed[None, :] == targets[:, None])
    chosen = jnp.sum(jnp.where(hit, index[None, :], 0), axis=1)
    return (keyed, live, chosen)


def call(kernel, out_shape, in_specs, args, flops=0, scratch=(), limit=16, out_specs=None):
    outs = jax.tree.leaves(out_shape)
    whole = [x for x, spec in zip(args, in_specs) if spec is not HBM]
    moved = sum(x.size * x.dtype.itemsize for x in whole + outs)
    return pl.pallas_call(
        kernel,
        out_shape=out_shape,
        in_specs=in_specs,
        out_specs=out_specs or jax.tree.map(lambda _: VMEM, out_shape),
        scratch_shapes=list(scratch),
        compiler_params=pltpu.CompilerParams(vmem_limit_bytes=limit * MIB),
        cost_estimate=pl.CostEstimate(flops=flops, bytes_accessed=moved, transcendentals=0),
    )(*args)


def pick_kernel(table_ref, source_ref, out_ref):
    def step(t, carry):
        wanted = table_ref[t]
        block = source_ref[jnp.maximum(wanted, 0)]
        out_ref[t] = jnp.where(wanted >= 0, block, jnp.zeros_like(block))
        return carry

    lax.fori_loop(0, out_ref.shape[0], step, 0, unroll=8)


def pick(source, table):
    shape = jax.ShapeDtypeStruct(table.shape + source.shape[1:], source.dtype)
    return call(pick_kernel, shape, [SMEM, VMEM], (table, source))


def put_pieces(out_ref, item, value, first=0):
    rows, cols = value.shape
    narrow = out_ref.shape[3]
    across = cols // narrow
    for i in range(rows // TILE_ROWS):
        for j in range(across):
            out_ref[(first + i) * across + j, item] = value[
                i * TILE_ROWS : (i + 1) * TILE_ROWS, j * narrow : (j + 1) * narrow
            ]


def unpack_kernel(pieces_ref, *out_refs):
    owners, count, tall, narrow = pieces_ref.shape
    for item in range(count):
        if len(out_refs) == 1:
            out_ref = out_refs[0].at[item]
        else:
            out_ref = out_refs[item]
        across = out_ref.shape[1] // narrow
        for i in range(owners // across):
            for j in range(across):
                out_ref[i * tall : (i + 1) * tall, j * narrow : (j + 1) * narrow] = pieces_ref[
                    i * across + j, item
                ]


def add_kernel(got_ref, piece_ref, out_ref):
    out_ref[...] = (got_ref[...].astype(F32) + piece_ref[...].astype(F32)).astype(BF16)


def after_kernel(*refs):
    source_ref, out_ref = refs[-2:]
    out_ref[...] = source_ref[...]


def pack_kernel(own_ref, *rest):
    got, out_ref = rest[:-1], rest[-1]
    count, rows = own_ref.shape[:2]
    part = got[0].shape[1]
    for item in range(count):
        for stream in range(rows // part):
            total = own_ref[item, stream * part : (stream + 1) * part].astype(F32)
            for ref in got[2 * stream : 2 * stream + 2]:
                total = total + ref[item].astype(F32)
            put_pieces(out_ref, item, total.astype(BF16), stream * part // TILE_ROWS)


def hop(value, step, ring):
    return lax.ppermute(value, "dp", [(i, (i + step) % ring) for i in range(ring)])


def chains(count, ring):
    far, near = ring // 2, ring - 1 - ring // 2
    for step in range(far):
        for block in range(count):
            long_way = 1 if block % 2 == 0 else -1
            for way, length in ((long_way, far), (-long_way, near)):
                place = step - (far - length)
                if place >= 0:
                    yield block, way, place, length


def sum_over_ring(blocks, rows, owners, root, tables):
    count, _, cols = blocks.shape
    ring = lax.axis_size("dp")
    me = lax.axis_index("dp").astype(jnp.int32)
    part = rows // STREAMS
    shape = (count, part, cols)
    order = list(chains(STREAMS, ring))

    def piece(me, stream, way, place, length):
        target = lax.rem(me + way * (length - place) + ring, ring)
        return lax.dynamic_slice(blocks, (0, target * rows + stream * part, 0), shape)

    first = {step[:2]: piece(me, *step) for step in order if step[2] == 0}
    later, first = lax.optimization_barrier((me, first))
    pieces = {step[:3]: piece(later, *step) for step in order if step[2] > 0}
    own = lax.dynamic_slice(blocks, (0, later * rows, 0), (count, rows, cols))
    held, sent = {}, {}
    for stream, way, place, length in order:
        if place == 0:
            value = first[stream, way]
        else:
            value = call(
                add_kernel,
                jax.ShapeDtypeStruct(shape, BF16),
                [VMEM, VMEM],
                (held[stream, way], pieces[stream, way, place]),
            )
        sent[stream, way] = value
        held[stream, way] = hop(value, way, ring)
    earlier = [held[key] if key != (0, 1) else sent[key] for key in held]
    after = jax.ShapeDtypeStruct(root.shape, root.dtype)
    earlier += tables
    root = call(after_kernel, after, [HBM] * len(earlier) + [VMEM], (*earlier, root))
    got = [held[stream, way] for stream in range(STREAMS) for way in (1, -1)]
    narrow = cols * (rows // TILE_ROWS) // owners
    packed = call(
        pack_kernel,
        jax.ShapeDtypeStruct((owners, count, TILE_ROWS, narrow), BF16),
        [VMEM] * (1 + len(got)),
        (own, *got),
    )
    return packed, root


def columns(me, k, ring, width):
    return pl.ds(pl.multiple_of(lax.rem(me + k, ring) * width, width), width)


def mix_kernel(ring, places, me_ref, root_ref, *rest):
    shards, (old_ref, new_ref) = rest[: len(places)], rest[len(places) :]
    me = me_ref[0]
    rows = root_ref.shape[1]
    for a in range(root_ref.shape[0]):
        total = old_ref[a]
        for (block, k), shard in zip(places, shards):
            if block == a:
                total = total + jnp.dot(
                    root_ref[a, :, columns(me, k, ring, rows)],
                    shard[...],
                    preferred_element_type=F32,
                )
        new_ref[a] = total


def gram_kernel(ring, places, me_ref, *rest):
    shards, rest = rest[: len(places)], rest[len(places) :]
    owned, (left_in, right_in, left_ref, right_ref) = rest[:-4], rest[-4:]
    me = me_ref[0]
    rows = left_ref.shape[1]
    mine = columns(me, 0, ring, rows)
    left_ref[...] = left_in[...]
    for a in range(left_ref.shape[0]):
        total = right_in[a]
        for (block, k), shard in zip(places, shards):
            if block == a:
                cols = columns(me, k, ring, rows)
                left_ref[a, :, cols] = left_ref[a, :, cols] + lax.dot_general(
                    owned[a][...],
                    shard[...],
                    (((1,), (1,)), ((), ())),
                    preferred_element_type=F32,
                )
                total = total + lax.dot_general(
                    shard[:, mine],
                    shard[...],
                    (((0,), (0,)), ((), ())),
                    preferred_element_type=F32,
                )
        right_ref[a] = total


def result_kernel(ring, places, me_ref, root_ref, right_ref, *rest):
    count = len(places)
    shards, (old_ref, out_ref), rest = rest[:count], rest[count : count + 2], rest[count + 2 :]
    kept, sems = rest[:count], rest[count]
    copies = []
    for i in range(count):
        copies.append(pltpu.make_async_copy(shards[i], kept[i], sems.at[i]))
        copies[i].start()
    me = me_ref[0]
    rows = root_ref.shape[1]
    for a in range(root_ref.shape[0]):
        total = old_ref[a]
        for (block, k), shard in zip(places, shards):
            if block == a:
                total = total + jnp.dot(
                    root_ref[a, :, columns(me, k, ring, rows)],
                    shard[...],
                    preferred_element_type=F32,
                )
        result = jnp.dot(total.astype(BF16), right_ref[a], preferred_element_type=F32)
        put_pieces(out_ref, a, result.astype(BF16))
    for copy in copies:
        copy.wait()


def swap(pieces):
    return lax.all_to_all(pieces, "own", split_axis=0, concat_axis=0, tiled=True)


def local(partials, active_mask, block_owner, left_stats, right_stats, left_root, right_root):
    blocks, width = partials.shape[1], partials.shape[3]
    active_count, rows = left_stats.shape[:2]
    owners = lax.axis_size("own")
    ring = lax.axis_size("dp")
    me = lax.axis_index("dp").astype(jnp.int32)[None]
    keyed, live, chosen = slot_table(active_mask, block_owner, active_count, owners)
    wanted = jnp.where(live, keyed, -1)

    summed, right_root = sum_over_ring(
        partials[0], rows, owners, right_root, [chosen, wanted]
    )
    right_full = lax.all_gather(right_root, "dp", axis=1, tiled=True)

    spread = swap(summed)
    piece = spread.shape[2:]
    picked = pick(spread.reshape((-1,) + piece), chosen)
    arrived = swap(picked.reshape((owners, active_count) + piece))
    slab = jax.ShapeDtypeStruct((rows, width), BF16)
    gradient = call(unpack_kernel, [slab] * active_count, [VMEM], (arrived,))
    gradient = list(gradient)

    flops = 2 * rows * rows * width
    slabs = jax.ShapeDtypeStruct((active_count, rows, width), F32)
    mixed = jnp.zeros(slabs.shape, F32)
    left_new, right_new = left_stats, right_stats

    def gram(places, shards, left, right):
        return call(
            functools.partial(gram_kernel, ring, places),
            [slabs, slabs],
            [SMEM] + [VMEM] * (len(shards) + active_count + 2),
            (me, *shards, *gradient, left, right),
            flops=2 * flops * len(shards),
        )

    held = {}
    places, shards = [(block, 0) for block in range(active_count)], list(gradient)
    for step in range(ring // 2):
        mixed = call(
            functools.partial(mix_kernel, ring, places),
            slabs,
            [SMEM, VMEM] + [VMEM] * (len(shards) + 1),
            (me, left_root, *shards, mixed),
            flops=flops * len(shards),
        )
        left_new, right_new = gram(places, shards, left_new, right_new)
        places, shards = [], []
        for block, way, place, length in chains(active_count, ring):
            if place == step:
                value = held.get((block, way), gradient[block])
                if step == ring // 2 - 1:
                    value, right_full = lax.optimization_barrier((value, right_full))
                held[block, way] = hop(value, way, ring)
                places.append((block, (-way * (place + 1)) % ring))
                shards.append(held[block, way])
    slab = jax.ShapeDtypeStruct((rows, width), BF16)
    result, *shards = call(
        functools.partial(result_kernel, ring, places),
        [jax.ShapeDtypeStruct((owners, active_count) + piece, BF16)] + [slab] * len(shards),
        [SMEM, VMEM, VMEM] + [VMEM] * (len(shards) + 1),
        (me, left_root, right_full, *shards, mixed),
        flops=flops * (len(shards) + ring * active_count),
        scratch=[pltpu.SemaphoreType.DMA((len(shards),))],
        limit=24,
        out_specs=[VMEM] + [HBM] * len(shards),
    )

    back = swap(result)
    placed = pick(back.reshape((-1,) + piece), wanted)
    returned = swap(placed.reshape((owners, blocks) + piece))
    preconditioned = call(
        unpack_kernel,
        jax.ShapeDtypeStruct((blocks, rows, width), BF16),
        [VMEM],
        (returned,),
    )

    left_new, right_new = gram(places, shards, left_new, right_new)
    return (preconditioned, left_new, right_new)


def solution(mesh):
    placed = (
        P("dp", "own", None, None),
        P(),
        P(),
        P("own", "dp", None),
        P("own", "dp", None),
        P("own", "dp", None),
        P("own", "dp", None),
    )
    return jax.shard_map(
        local,
        mesh=mesh,
        in_specs=placed,
        out_specs=(P("own", "dp", None), P("own", "dp", None), P("own", "dp", None)),
        check_vma=False,
    )
```

```python
import functools

import jax
import jax.numpy as jnp
from jax import lax
from jax.experimental import pallas as pl
from jax.experimental.pallas import tpu as pltpu
from jax.sharding import PartitionSpec as P

TILE_ROWS = 16
F32 = jnp.float32
BF16 = jnp.bfloat16
MIB = 1024 * 1024
VMEM = pl.BlockSpec(memory_space=pltpu.VMEM)
SMEM = pl.BlockSpec(memory_space=pltpu.SMEM)
HBM = pl.BlockSpec(memory_space=pltpu.HBM)


def slot_table(active_mask, block_owner, active_count, owners):
    block_total = active_mask.shape[0]
    index = jnp.arange(block_total, dtype=jnp.int32)
    live = active_mask == 1
    earlier = (
        (block_owner[:, None] == block_owner[None, :])
        & live[None, :]
        & (index[None, :] < index[:, None])
    )
    slots = jnp.sum(earlier.astype(jnp.int32), axis=1)
    keyed = jnp.where(live, block_owner * active_count + slots, 0)
    targets = jnp.arange(owners * active_count, dtype=jnp.int32)
    hit = live[None, :] & (keyed[None, :] == targets[:, None])
    chosen = jnp.sum(jnp.where(hit, index[None, :], 0), axis=1)
    return (keyed, live, chosen)


def call(kernel, out_shape, in_specs, args, flops=0, scratch=(), limit=16, out_specs=None):
    outs = jax.tree.leaves(out_shape)
    whole = [x for x, spec in zip(args, in_specs) if spec is not HBM]
    moved = sum(x.size * x.dtype.itemsize for x in whole + outs)
    return pl.pallas_call(
        kernel,
        out_shape=out_shape,
        in_specs=in_specs,
        out_specs=out_specs or jax.tree.map(lambda _: VMEM, out_shape),
        scratch_shapes=list(scratch),
        compiler_params=pltpu.CompilerParams(vmem_limit_bytes=limit * MIB),
        cost_estimate=pl.CostEstimate(flops=flops, bytes_accessed=moved, transcendentals=0),
    )(*args)


def pick_kernel(table_ref, source_ref, out_ref):
    def step(t, carry):
        wanted = table_ref[t]
        block = source_ref[jnp.maximum(wanted, 0)]
        out_ref[t] = jnp.where(wanted >= 0, block, jnp.zeros_like(block))
        return carry

    lax.fori_loop(0, out_ref.shape[0], step, 0, unroll=8)


def pick(source, table):
    shape = jax.ShapeDtypeStruct(table.shape + source.shape[1:], source.dtype)
    return call(pick_kernel, shape, [SMEM, VMEM], (table, source))


def put_pieces(out_ref, item, value, first=0):
    rows, cols = value.shape
    narrow = out_ref.shape[3]
    across = cols // narrow
    for i in range(rows // TILE_ROWS):
        for j in range(across):
            out_ref[(first + i) * across + j, item] = value[
                i * TILE_ROWS : (i + 1) * TILE_ROWS, j * narrow : (j + 1) * narrow
            ]


def unpack_kernel(pieces_ref, *out_refs):
    owners, count, tall, narrow = pieces_ref.shape
    for item in range(count):
        if len(out_refs) == 1:
            out_ref = out_refs[0].at[item]
        else:
            out_ref = out_refs[item]
        across = out_ref.shape[1] // narrow
        for i in range(owners // across):
            for j in range(across):
                out_ref[i * tall : (i + 1) * tall, j * narrow : (j + 1) * narrow] = pieces_ref[
                    i * across + j, item
                ]


def add_kernel(got_ref, piece_ref, out_ref):
    out_ref[...] = (got_ref[...].astype(F32) + piece_ref[...].astype(F32)).astype(BF16)


def after_kernel(*refs):
    source_ref, out_ref = refs[-2:]
    out_ref[...] = source_ref[...]


def pack_kernel(own_ref, *rest):
    got, out_ref = rest[:-1], rest[-1]
    for item in range(own_ref.shape[0]):
        total = own_ref[item].astype(F32)
        for ref in got[2 * item : 2 * item + 2]:
            total = total + ref[0].astype(F32)
        put_pieces(out_ref, item, total.astype(BF16))


def hop(value, step, ring):
    return lax.ppermute(value, "dp", [(i, (i + step) % ring) for i in range(ring)])


def chains(count, ring):
    far, near = ring // 2, ring - 1 - ring // 2
    for step in range(far):
        for block in range(count):
            long_way = 1 if block % 2 == 0 else -1
            for way, length in ((long_way, far), (-long_way, near)):
                place = step - (far - length)
                if place >= 0:
                    yield block, way, place, length


def sum_over_ring(blocks, rows, owners, root, tables):
    count, _, cols = blocks.shape
    ring = lax.axis_size("dp")
    me = lax.axis_index("dp").astype(jnp.int32)
    shape = (1, rows, cols)
    order = list(chains(count, ring))

    def piece(me, stream, way, place, length):
        target = lax.rem(me + way * (length - place) + ring, ring)
        return lax.dynamic_slice(blocks, (stream, target * rows, 0), shape)

    first = {step[:2]: piece(me, *step) for step in order if step[2] == 0}
    later, first = lax.optimization_barrier((me, first))
    pieces = {step[:3]: piece(later, *step) for step in order if step[2] > 0}
    own = lax.dynamic_slice(blocks, (0, later * rows, 0), (count, rows, cols))
    held, sent = {}, {}
    for stream, way, place, length in order:
        if place == 0:
            value = first[stream, way]
        else:
            value = call(
                add_kernel,
                jax.ShapeDtypeStruct(shape, BF16),
                [VMEM, VMEM],
                (held[stream, way], pieces[stream, way, place]),
            )
        sent[stream, way] = value
        held[stream, way] = hop(value, way, ring)
    earlier = [held[key] if key != (0, 1) else sent[key] for key in held]
    after = jax.ShapeDtypeStruct(root.shape, root.dtype)
    earlier += tables
    root = call(after_kernel, after, [HBM] * len(earlier) + [VMEM], (*earlier, root))
    got = [held[stream, way] for stream in range(count) for way in (1, -1)]
    narrow = cols * (rows // TILE_ROWS) // owners
    packed = call(
        pack_kernel,
        jax.ShapeDtypeStruct((owners, count, TILE_ROWS, narrow), BF16),
        [VMEM] * (1 + len(got)),
        (own, *got),
    )
    return packed, root


def columns(me, k, ring, width):
    return pl.ds(pl.multiple_of(lax.rem(me + k, ring) * width, width), width)


def mix_kernel(ring, places, me_ref, root_ref, *rest):
    shards, (old_ref, new_ref) = rest[: len(places)], rest[len(places) :]
    me = me_ref[0]
    rows = root_ref.shape[1]
    for a in range(root_ref.shape[0]):
        total = old_ref[a]
        for (block, k), shard in zip(places, shards):
            if block == a:
                total = total + jnp.dot(
                    root_ref[a, :, columns(me, k, ring, rows)],
                    shard[...],
                    preferred_element_type=F32,
                )
        new_ref[a] = total


def gram_kernel(ring, places, me_ref, *rest):
    shards, rest = rest[: len(places)], rest[len(places) :]
    owned, (left_in, right_in, left_ref, right_ref) = rest[:-4], rest[-4:]
    me = me_ref[0]
    rows = left_ref.shape[1]
    mine = columns(me, 0, ring, rows)
    left_ref[...] = left_in[...]
    for a in range(left_ref.shape[0]):
        total = right_in[a]
        for (block, k), shard in zip(places, shards):
            if block == a:
                cols = columns(me, k, ring, rows)
                left_ref[a, :, cols] = left_ref[a, :, cols] + lax.dot_general(
                    owned[a][...],
                    shard[...],
                    (((1,), (1,)), ((), ())),
                    preferred_element_type=F32,
                )
                total = total + lax.dot_general(
                    shard[:, mine],
                    shard[...],
                    (((0,), (0,)), ((), ())),
                    preferred_element_type=F32,
                )
        right_ref[a] = total


def result_kernel(ring, places, me_ref, root_ref, right_ref, *rest):
    count = len(places)
    shards, (old_ref, out_ref), rest = rest[:count], rest[count : count + 2], rest[count + 2 :]
    kept, sems = rest[:count], rest[count]
    copies = []
    for i in range(count):
        copies.append(pltpu.make_async_copy(shards[i], kept[i], sems.at[i]))
        copies[i].start()
    me = me_ref[0]
    rows = root_ref.shape[1]
    for a in range(root_ref.shape[0]):
        total = old_ref[a]
        for (block, k), shard in zip(places, shards):
            if block == a:
                total = total + jnp.dot(
                    root_ref[a, :, columns(me, k, ring, rows)],
                    shard[...],
                    preferred_element_type=F32,
                )
        result = jnp.dot(total.astype(BF16), right_ref[a], preferred_element_type=F32)
        put_pieces(out_ref, a, result.astype(BF16))
    for copy in copies:
        copy.wait()


def swap(pieces):
    return lax.all_to_all(pieces, "own", split_axis=0, concat_axis=0, tiled=True)


def local(partials, active_mask, block_owner, left_stats, right_stats, left_root, right_root):
    blocks, width = partials.shape[1], partials.shape[3]
    active_count, rows = left_stats.shape[:2]
    owners = lax.axis_size("own")
    ring = lax.axis_size("dp")
    me = lax.axis_index("dp").astype(jnp.int32)[None]
    keyed, live, chosen = slot_table(active_mask, block_owner, active_count, owners)
    wanted = jnp.where(live, keyed, -1)

    summed, right_root = sum_over_ring(
        partials[0], rows, owners, right_root, [chosen, wanted]
    )
    right_full = lax.all_gather(right_root, "dp", axis=1, tiled=True)

    spread = swap(summed)
    piece = spread.shape[2:]
    picked = pick(spread.reshape((-1,) + piece), chosen)
    arrived = swap(picked.reshape((owners, active_count) + piece))
    slab = jax.ShapeDtypeStruct((rows, width), BF16)
    gradient = call(unpack_kernel, [slab] * active_count, [VMEM], (arrived,))
    gradient = list(gradient)

    flops = 2 * rows * rows * width
    slabs = jax.ShapeDtypeStruct((active_count, rows, width), F32)
    mixed = jnp.zeros(slabs.shape, F32)
    left_new, right_new = left_stats, right_stats

    def gram(places, shards, left, right):
        return call(
            functools.partial(gram_kernel, ring, places),
            [slabs, slabs],
            [SMEM] + [VMEM] * (len(shards) + active_count + 2),
            (me, *shards, *gradient, left, right),
            flops=2 * flops * len(shards),
        )

    held = {}
    places, shards = [(block, 0) for block in range(active_count)], list(gradient)
    for step in range(ring // 2):
        mixed = call(
            functools.partial(mix_kernel, ring, places),
            slabs,
            [SMEM, VMEM] + [VMEM] * (len(shards) + 1),
            (me, left_root, *shards, mixed),
            flops=flops * len(shards),
        )
        left_new, right_new = gram(places, shards, left_new, right_new)
        places, shards = [], []
        for block, way, place, length in chains(active_count, ring):
            if place == step:
                value = held.get((block, way), gradient[block])
                if step == ring // 2 - 1:
                    value, right_full = lax.optimization_barrier((value, right_full))
                held[block, way] = hop(value, way, ring)
                places.append((block, (-way * (place + 1)) % ring))
                shards.append(held[block, way])
    slab = jax.ShapeDtypeStruct((rows, width), BF16)
    result, *shards = call(
        functools.partial(result_kernel, ring, places),
        [jax.ShapeDtypeStruct((owners, active_count) + piece, BF16)] + [slab] * len(shards),
        [SMEM, VMEM, VMEM] + [VMEM] * (len(shards) + 1),
        (me, left_root, right_full, *shards, mixed),
        flops=flops * (len(shards) + ring * active_count),
        scratch=[pltpu.SemaphoreType.DMA((len(shards),))],
        limit=24,
        out_specs=[VMEM] + [HBM] * len(shards),
    )

    back = swap(result)
    placed = pick(back.reshape((-1,) + piece), wanted)
    returned = swap(placed.reshape((owners, blocks) + piece))
    preconditioned = call(
        unpack_kernel,
        jax.ShapeDtypeStruct((blocks, rows, width), BF16),
        [VMEM],
        (returned,),
    )

    left_new, right_new = gram(places, shards, left_new, right_new)
    return (preconditioned, left_new, right_new)


def solution(mesh):
    placed = (
        P("dp", "own", None, None),
        P(),
        P(),
        P("own", "dp", None),
        P("own", "dp", None),
        P("own", "dp", None),
        P("own", "dp", None),
    )
    return jax.shard_map(
        local,
        mesh=mesh,
        in_specs=placed,
        out_specs=(P("own", "dp", None), P("own", "dp", None), P("own", "dp", None)),
        check_vma=False,
    )
```

```python
import functools

import jax
import jax.numpy as jnp
from jax import lax
from jax.experimental import pallas as pl
from jax.experimental.pallas import tpu as pltpu
from jax.sharding import PartitionSpec as P

TILE_ROWS = 16
F32 = jnp.float32
BF16 = jnp.bfloat16
MIB = 1024 * 1024
VMEM = pl.BlockSpec(memory_space=pltpu.VMEM)
SMEM = pl.BlockSpec(memory_space=pltpu.SMEM)
HBM = pl.BlockSpec(memory_space=pltpu.HBM)


def slot_table(active_mask, block_owner, active_count, owners):
    block_total = active_mask.shape[0]
    index = jnp.arange(block_total, dtype=jnp.int32)
    live = active_mask == 1
    earlier = (
        (block_owner[:, None] == block_owner[None, :])
        & live[None, :]
        & (index[None, :] < index[:, None])
    )
    slots = jnp.sum(earlier.astype(jnp.int32), axis=1)
    keyed = jnp.where(live, block_owner * active_count + slots, 0)
    targets = jnp.arange(owners * active_count, dtype=jnp.int32)
    hit = live[None, :] & (keyed[None, :] == targets[:, None])
    chosen = jnp.sum(jnp.where(hit, index[None, :], 0), axis=1)
    return (keyed, live, chosen)


def call(kernel, out_shape, in_specs, args, flops=0, scratch=(), limit=16, out_specs=None):
    outs = jax.tree.leaves(out_shape)
    whole = [x for x, spec in zip(args, in_specs) if spec is not HBM]
    moved = sum(x.size * x.dtype.itemsize for x in whole + outs)
    return pl.pallas_call(
        kernel,
        out_shape=out_shape,
        in_specs=in_specs,
        out_specs=out_specs or jax.tree.map(lambda _: VMEM, out_shape),
        scratch_shapes=list(scratch),
        compiler_params=pltpu.CompilerParams(vmem_limit_bytes=limit * MIB),
        cost_estimate=pl.CostEstimate(flops=flops, bytes_accessed=moved, transcendentals=0),
    )(*args)


def pick_kernel(table_ref, source_ref, out_ref):
    def step(t, carry):
        wanted = table_ref[t]
        block = source_ref[jnp.maximum(wanted, 0)]
        out_ref[t] = jnp.where(wanted >= 0, block, jnp.zeros_like(block))
        return carry

    lax.fori_loop(0, out_ref.shape[0], step, 0, unroll=8)


def pick(source, table):
    shape = jax.ShapeDtypeStruct(table.shape + source.shape[1:], source.dtype)
    return call(pick_kernel, shape, [SMEM, VMEM], (table, source))


def put_pieces(out_ref, item, value, first=0):
    rows, cols = value.shape
    narrow = out_ref.shape[3]
    across = cols // narrow
    for i in range(rows // TILE_ROWS):
        for j in range(across):
            out_ref[(first + i) * across + j, item] = value[
                i * TILE_ROWS : (i + 1) * TILE_ROWS, j * narrow : (j + 1) * narrow
            ]


def unpack_kernel(pieces_ref, *out_refs):
    owners, count, tall, narrow = pieces_ref.shape
    for item in range(count):
        if len(out_refs) == 1:
            out_ref = out_refs[0].at[item]
        else:
            out_ref = out_refs[item]
        across = out_ref.shape[1] // narrow
        for i in range(owners // across):
            for j in range(across):
                out_ref[i * tall : (i + 1) * tall, j * narrow : (j + 1) * narrow] = pieces_ref[
                    i * across + j, item
                ]


def add_kernel(got_ref, piece_ref, out_ref):
    out_ref[...] = (got_ref[...].astype(F32) + piece_ref[...].astype(F32)).astype(BF16)


def after_kernel(*refs):
    source_ref, out_ref = refs[-2:]
    out_ref[...] = source_ref[...]


def pack_kernel(own_ref, *rest):
    got, out_ref = rest[:-1], rest[-1]
    for item in range(own_ref.shape[0]):
        total = own_ref[item].astype(F32)
        for ref in got[2 * item : 2 * item + 2]:
            total = total + ref[0].astype(F32)
        put_pieces(out_ref, item, total.astype(BF16))


def hop(value, step, ring):
    return lax.ppermute(value, "dp", [(i, (i + step) % ring) for i in range(ring)])


def chains(count, ring):
    far, near = ring // 2, ring - 1 - ring // 2
    for step in range(far):
        for block in range(count):
            long_way = 1 if block % 2 == 0 else -1
            for way, length in ((long_way, far), (-long_way, near)):
                place = step - (far - length)
                if place >= 0:
                    yield block, way, place, length


def sum_over_ring(blocks, rows, owners, root, tables):
    count, _, cols = blocks.shape
    ring = lax.axis_size("dp")
    me = lax.axis_index("dp").astype(jnp.int32)
    shape = (1, rows, cols)
    order = list(chains(count, ring))

    def piece(me, stream, way, place, length):
        target = lax.rem(me + way * (length - place) + ring, ring)
        return lax.dynamic_slice(blocks, (stream, target * rows, 0), shape)

    first = {step[:2]: piece(me, *step) for step in order if step[2] == 0}
    later, first = lax.optimization_barrier((me, first))
    pieces = {step[:3]: piece(later, *step) for step in order if step[2] > 0}
    own = lax.dynamic_slice(blocks, (0, later * rows, 0), (count, rows, cols))
    held, sent = {}, {}
    for stream, way, place, length in order:
        if place == 0:
            value = first[stream, way]
        else:
            value = call(
                add_kernel,
                jax.ShapeDtypeStruct(shape, BF16),
                [VMEM, VMEM],
                (held[stream, way], pieces[stream, way, place]),
            )
        sent[stream, way] = value
        held[stream, way] = hop(value, way, ring)
    earlier = [held[key] if key not in ((0, 1), (1, -1)) else sent[key] for key in held]
    after = jax.ShapeDtypeStruct(root.shape, root.dtype)
    earlier += tables
    root = call(after_kernel, after, [HBM] * len(earlier) + [VMEM], (*earlier, root))
    got = [held[stream, way] for stream in range(count) for way in (1, -1)]
    narrow = cols * (rows // TILE_ROWS) // owners
    packed = call(
        pack_kernel,
        jax.ShapeDtypeStruct((owners, count, TILE_ROWS, narrow), BF16),
        [VMEM] * (1 + len(got)),
        (own, *got),
    )
    return packed, root


def columns(me, k, ring, width):
    return pl.ds(pl.multiple_of(lax.rem(me + k, ring) * width, width), width)


def mix_kernel(ring, places, me_ref, root_ref, *rest):
    shards, (old_ref, new_ref) = rest[: len(places)], rest[len(places) :]
    me = me_ref[0]
    rows = root_ref.shape[1]
    for a in range(root_ref.shape[0]):
        total = old_ref[a]
        for (block, k), shard in zip(places, shards):
            if block == a:
                total = total + jnp.dot(
                    root_ref[a, :, columns(me, k, ring, rows)],
                    shard[...],
                    preferred_element_type=F32,
                )
        new_ref[a] = total


def gram_kernel(ring, places, me_ref, *rest):
    shards, rest = rest[: len(places)], rest[len(places) :]
    owned, (left_in, right_in, left_ref, right_ref) = rest[:-4], rest[-4:]
    me = me_ref[0]
    rows = left_ref.shape[1]
    mine = columns(me, 0, ring, rows)
    left_ref[...] = left_in[...]
    for a in range(left_ref.shape[0]):
        total = right_in[a]
        for (block, k), shard in zip(places, shards):
            if block == a:
                cols = columns(me, k, ring, rows)
                left_ref[a, :, cols] = left_ref[a, :, cols] + lax.dot_general(
                    owned[a][...],
                    shard[...],
                    (((1,), (1,)), ((), ())),
                    preferred_element_type=F32,
                )
                total = total + lax.dot_general(
                    shard[:, mine],
                    shard[...],
                    (((0,), (0,)), ((), ())),
                    preferred_element_type=F32,
                )
        right_ref[a] = total


def result_kernel(ring, places, me_ref, root_ref, right_ref, *rest):
    count = len(places)
    shards, (old_ref, out_ref), rest = rest[:count], rest[count : count + 2], rest[count + 2 :]
    kept, sems = rest[:count], rest[count]
    copies = []
    for i in range(count):
        copies.append(pltpu.make_async_copy(shards[i], kept[i], sems.at[i]))
        copies[i].start()
    me = me_ref[0]
    rows = root_ref.shape[1]
    for a in range(root_ref.shape[0]):
        total = old_ref[a]
        for (block, k), shard in zip(places, shards):
            if block == a:
                total = total + jnp.dot(
                    root_ref[a, :, columns(me, k, ring, rows)],
                    shard[...],
                    preferred_element_type=F32,
                )
        factor = right_ref[:, a].reshape(ring * rows, right_ref.shape[3])
        result = jnp.dot(total.astype(BF16), factor, preferred_element_type=F32)
        put_pieces(out_ref, a, result.astype(BF16))
    for copy in copies:
        copy.wait()


def swap(pieces):
    return lax.all_to_all(pieces, "own", split_axis=0, concat_axis=0, tiled=True)


def local(partials, active_mask, block_owner, left_stats, right_stats, left_root, right_root):
    blocks, width = partials.shape[1], partials.shape[3]
    active_count, rows = left_stats.shape[:2]
    owners = lax.axis_size("own")
    ring = lax.axis_size("dp")
    me = lax.axis_index("dp").astype(jnp.int32)[None]
    keyed, live, chosen = slot_table(active_mask, block_owner, active_count, owners)
    wanted = jnp.where(live, keyed, -1)

    summed, right_root = sum_over_ring(
        partials[0], rows, owners, right_root, [chosen, wanted]
    )
    right_full = lax.all_gather(right_root, "dp", axis=0)

    spread = swap(summed)
    piece = spread.shape[2:]
    picked = pick(spread.reshape((-1,) + piece), chosen)
    arrived = swap(picked.reshape((owners, active_count) + piece))
    slab = jax.ShapeDtypeStruct((rows, width), BF16)
    gradient = call(unpack_kernel, [slab] * active_count, [VMEM], (arrived,))
    gradient = list(gradient)

    flops = 2 * rows * rows * width
    slabs = jax.ShapeDtypeStruct((active_count, rows, width), F32)
    mixed = jnp.zeros(slabs.shape, F32)
    left_new, right_new = left_stats, right_stats

    def gram(places, shards, left, right):
        return call(
            functools.partial(gram_kernel, ring, places),
            [slabs, slabs],
            [SMEM] + [VMEM] * (len(shards) + active_count + 2),
            (me, *shards, *gradient, left, right),
            flops=2 * flops * len(shards),
        )

    held = {}
    places, shards = [(block, 0) for block in range(active_count)], list(gradient)
    for step in range(ring // 2):
        mixed = call(
            functools.partial(mix_kernel, ring, places),
            slabs,
            [SMEM, VMEM] + [VMEM] * (len(shards) + 1),
            (me, left_root, *shards, mixed),
            flops=flops * len(shards),
        )
        left_new, right_new = gram(places, shards, left_new, right_new)
        places, shards = [], []
        for block, way, place, length in chains(active_count, ring):
            if place == step:
                value = held.get((block, way), gradient[block])
                if step == ring // 2 - 1:
                    value, right_full = lax.optimization_barrier((value, right_full))
                held[block, way] = hop(value, way, ring)
                places.append((block, (-way * (place + 1)) % ring))
                shards.append(held[block, way])
    slab = jax.ShapeDtypeStruct((rows, width), BF16)
    result, *shards = call(
        functools.partial(result_kernel, ring, places),
        [jax.ShapeDtypeStruct((owners, active_count) + piece, BF16)] + [slab] * len(shards),
        [SMEM, VMEM, VMEM] + [VMEM] * (len(shards) + 1),
        (me, left_root, right_full, *shards, mixed),
        flops=flops * (len(shards) + ring * active_count),
        scratch=[pltpu.SemaphoreType.DMA((len(shards),))],
        limit=24,
        out_specs=[VMEM] + [HBM] * len(shards),
    )

    back = swap(result)
    placed = pick(back.reshape((-1,) + piece), wanted)
    returned = swap(placed.reshape((owners, blocks) + piece))
    preconditioned = call(
        unpack_kernel,
        jax.ShapeDtypeStruct((blocks, rows, width), BF16),
        [VMEM],
        (returned,),
    )

    left_new, right_new = gram(places, shards, left_new, right_new)
    return (preconditioned, left_new, right_new)


def solution(mesh):
    placed = (
        P("dp", "own", None, None),
        P(),
        P(),
        P("own", "dp", None),
        P("own", "dp", None),
        P("own", "dp", None),
        P("own", "dp", None),
    )
    return jax.shard_map(
        local,
        mesh=mesh,
        in_specs=placed,
        out_specs=(P("own", "dp", None), P("own", "dp", None), P("own", "dp", None)),
        check_vma=False,
    )
```
